32 devices in a mesh: fib: 4 (over y, x), rest: 8 (over z, core).
Axes of the slice: x: 2, y: 2, z: 4, core: 2. Of those that a mesh axis runs over, the one named last changes fastest.
Arguments:
- tensor: float32 [32, 32, 64, 1024], P('fib', 'rest'), may hold values from -24 to 24
- factor_one: float32 [1024, 128], replicated, may hold values from 0 to 0.05
- factor_two: float32 [32, 128], P('fib'), may hold values from 0.05 to 0.35
- factor_three: float32 [32, 128], P('rest'), may hold values from 0.03 to 0.25
- factor_four: float32 [64, 128], replicated, may hold values from 0.03 to 0.25
Outputs:
- new_factor: float32 [1024, 128], replicated
- factor_gram: float32 [128, 128], replicated
The draws below stay inside these ranges and needn't reach their ends.
All inputs are finite; a program needn't handle non-finite values.
Results may differ from the reference program's by a relative error of at most 0.00014.
Values sent between devices are 32-bit elements; how exact they have to be, the bound alone decides.
A program may use at most 64 MiB of HBM per device.

```python
import jax
import jax.numpy as jnp
from jax import lax

RANK = 128
MODE1 = 1024
MODE4 = 64
MODE2 = 32
MODE3 = 32


def strengthened(values, own_key, source, target, shards_of, factor):
    def block_of(position):
        return (jnp.arange(values.shape[position]) // (values.shape[position] // shards_of)).reshape((-1,) + (1,) * (values.ndim - 1 - position))

    near = jax.random.permutation(own_key, shards_of)[block_of(target)]
    second = (block_of(target) + shards_of // 2) % shards_of
    return jnp.where((block_of(source) == near) | (block_of(source) == second), factor * values, values)


def levels(stream_key, shape, pieces, low, top_value):
    factor_of = 1.0
    for position, blocks in pieces:
        heights = jax.random.uniform(jax.random.fold_in(jax.random.fold_in(stream_key, 6), position), (blocks,), jnp.float32, low / len(pieces), top_value / len(pieces))
        factor_of = factor_of * jnp.repeat(jnp.exp(heights), shape[position] // blocks).reshape((-1,) + (1,) * (len(shape) - 1 - position))
    return factor_of


def gaussian_with(stream_key, extent, spread, reach, shards, heavy, dtype=jnp.bfloat16):
    entries = spread * jax.random.normal(stream_key, extent, jnp.float32)
    if shards:
        entries = entries * levels(stream_key, extent, shards, -0.22, 0.18)
    return jnp.clip(strengthened(entries, jax.random.fold_in(stream_key, 3), *heavy), -reach, reach).astype(dtype)


def setup_inputs(seed: int = 0) -> dict:
    streams_of = jax.random.split(jax.random.key(seed), 6)
    return {
        "tensor": gaussian_with(streams_of[0], (MODE2, MODE3, MODE4, MODE1), 4.0, 24.0, ((0, 4), (1, 8)), (1, 3, 8, 2.0), jnp.float32),
        "factor_one": jnp.clip(jax.random.uniform(streams_of[1], (MODE1, RANK), jnp.float32, 0.0, 0.05), 0.0, 0.05),
        "factor_two": jnp.clip(0.05 + 0.29999999 * jax.random.uniform(streams_of[2], (MODE2, RANK), jnp.float32) ** levels(streams_of[2], (MODE2, RANK), ((0, 4),), -0.2, 0.2), 0.05, 0.35),
        "factor_three": jnp.clip(0.03 + 0.22 * jax.random.uniform(streams_of[3], (MODE3, RANK), jnp.float32) ** levels(streams_of[3], (MODE3, RANK), ((0, 8),), -0.2, 0.2), 0.03, 0.25),
        "factor_four": jnp.clip(jax.random.uniform(streams_of[4], (MODE4, RANK), jnp.float32, 0.03, 0.25), 0.03, 0.25),
    }


def hals_columns(factor, mttkrp, gram_v):
    highest = lax.Precision.HIGHEST
    rank_cols = factor.shape[1]
    width = 16 if rank_cols % 16 == 0 else rank_cols
    current = factor
    for block_idx in range(rank_cols // width):
        lower = block_idx * width
        base = jnp.dot(current, gram_v[:, lower:lower + width], precision=highest)
        old_cols = current[:, lower:lower + width]
        inner = gram_v[lower:lower + width, lower:lower + width]
        target = mttkrp[:, lower:lower + width]

        def update(k, cols):
            index = k.astype(jnp.int32)
            zero = jnp.zeros((), jnp.int32)
            inner_col = lax.dynamic_slice_in_dim(inner, index, 1, 1)
            diag = lax.dynamic_slice_in_dim(inner_col, index, 1, 0)[0, 0]
            product = lax.dynamic_slice_in_dim(base, index, 1, 1)[:, 0] + jnp.dot(cols - old_cols, inner_col, precision=highest)[:, 0]
            goal = lax.dynamic_slice_in_dim(target, index, 1, 1)[:, 0]
            column = lax.dynamic_slice_in_dim(cols, index, 1, 1)[:, 0]
            fresh = jnp.maximum(column + (goal - product) / diag, 0.0)
            return lax.dynamic_update_slice(cols, fresh[:, None], (zero, index))

        cols = lax.fori_loop(0, width, update, old_cols)
        current = current.at[:, lower:lower + width].set(cols)
    return current


def reference(tensor, factor_one, factor_two, factor_three, factor_four):
    highest = lax.Precision.HIGHEST

    def accumulate(total, pair):
        block, row_two = pair
        khatri = (row_two[None, None, :] * factor_three[:, None, :] * factor_four[None, :, :]).reshape(-1, RANK)
        flat = block.reshape(-1, MODE1)
        part = lax.dot_general(flat, khatri, (((0,), (0,)), ((), ())), precision=highest)
        return total + part, None

    mttkrp, _ = lax.scan(accumulate, jnp.zeros((MODE1, RANK), jnp.float32), (tensor, factor_two))
    gram_two = jnp.dot(factor_two.T, factor_two, precision=highest)
    gram_three = jnp.dot(factor_three.T, factor_three, precision=highest)
    gram_four = jnp.dot(factor_four.T, factor_four, precision=highest)
    gram_v = gram_two * gram_three * gram_four
    new_factor = hals_columns(factor_one, mttkrp, gram_v)
    factor_gram = jnp.dot(new_factor.T, new_factor, precision=highest)
    return new_factor, factor_gram
```

```python
import functools

import jax
import jax.numpy as jnp
from jax import lax
from jax.experimental import pallas as pl
from jax.experimental.pallas import tpu as pltpu
from jax.sharding import PartitionSpec as P

MESH = pl.DeviceIdType.MESH
HIGHEST = lax.Precision.HIGHEST
LANES = 128
BLOCK = 8


def split_bf16(value):
    high = value.astype(jnp.bfloat16)
    low = (value - high.astype(jnp.float32)).astype(jnp.bfloat16)
    return high, low


def gram_of(rows):
    return lax.dot_general(
        rows, rows, (((0,), (0,)), ((), ())),
        precision=HIGHEST, preferred_element_type=jnp.float32,
    )


def kernel(
    cfg, tensor, factor_one, factor_two, factor_three, factor_four, out, gram_out,
    tbuf, xown, khatri_t, two_all, three_all, three_cat, part, recv_core, sum_core,
    recv_fib, sum_fib, recv_z, mine, scaled, spread, fresh, flat,
    tensor_sem, xown_sem, two_send, two_recv, three_send, three_recv,
    core_send, core_recv, fib_send, fib_recv, z_send, z_recv,
    gz_send, gz_recv, gf_send, gf_recv, gc_send, gc_recv,
):
    nfib, nrest, nz, chunks, piece = cfg
    rank = factor_two.shape[1]
    fib = lax.axis_index("fib")
    rest = lax.axis_index("rest")
    core = rest % 2
    z = rest // 2
    other = 1 - core
    width = tensor.shape[1] // chunks
    pieces = nfib * nz
    nblocks = rank // BLOCK

    def remote(src, dst, send, recv, fib_to, rest_to):
        return pltpu.make_async_remote_copy(
            src_ref=src, dst_ref=dst, send_sem=send, recv_sem=recv,
            device_id=(fib_to, rest_to), device_id_type=MESH,
        )

    loads = []
    for chunk in range(chunks):
        copy = pltpu.make_async_copy(
            tensor.at[:, pl.ds(chunk * width, width)], tbuf.at[chunk], tensor_sem.at[chunk]
        )
        copy.start()
        loads.append(copy)
    xown_copy = pltpu.make_async_copy(factor_one.at[:, core, fib, z], xown, xown_sem)
    xown_copy.start()

    barrier = pltpu.get_barrier_semaphore()
    for d in range(1, nfib):
        pl.semaphore_signal(barrier, inc=1, device_id=((fib + d) % nfib, rest), device_id_type=MESH)
    for d in range(1, nrest):
        pl.semaphore_signal(barrier, inc=1, device_id=(fib, (rest + d) % nrest), device_id_type=MESH)

    two = factor_two[...]
    three = factor_three[...]
    four = factor_four[...]
    rows_two, rows_three, rows_four = two.shape[0], three.shape[0], four.shape[0]
    for i2 in range(rows_two):
        tile = jnp.concatenate(
            [(two[i2 : i2 + 1] * three[i3 : i3 + 1]) * four for i3 in range(rows_three)], axis=0
        )
        high, low = split_bf16(tile.T)
        span = rows_three * rows_four
        khatri_t[0:rank, i2 * span : (i2 + 1) * span] = high
        khatri_t[rank : 2 * rank, i2 * span : (i2 + 1) * span] = low

    two_all[fib] = two
    three_all[rest] = three
    pl.semaphore_wait(barrier, nfib - 1 + nrest - 1)
    small = []
    for d in range(1, nfib):
        small.append(remote(two_all.at[fib], two_all.at[fib], two_send.at[d], two_recv.at[d], (fib + d) % nfib, rest))
    for d in range(1, nrest):
        small.append(remote(three_all.at[rest], three_all.at[rest], three_send.at[d], three_recv.at[d], fib, (rest + d) % nrest))
    for copy in small:
        copy.start()

    sends = list(small)

    def multiply(chunk):
        loads[chunk].wait()
        depth = tbuf.shape[1]
        step = min(depth, 512)
        total = None
        for k in range(0, depth, step):
            high, low = split_bf16(tbuf[chunk, k : k + step, :])
            weights = khatri_t[:, k : k + step]
            term = jnp.dot(weights, high, preferred_element_type=jnp.float32)
            term = term + jnp.dot(weights, low, preferred_element_type=jnp.float32)
            total = term if total is None else total + term
        value = (total[0:rank] + total[rank : 2 * rank]).T
        if piece % 8 == 0:
            part[chunk] = value.reshape(2 * pieces, piece, rank)
        else:
            for p in range(2 * pieces):
                part[chunk, p] = value[p * piece : (p + 1) * piece]

    core_copies, fib_copies, z_copies = {}, {}, {}

    def start_core(chunk):
        copy = remote(
            part.at[chunk, pl.ds(other * pieces, pieces)], recv_core.at[chunk],
            core_send.at[chunk], core_recv.at[chunk], fib, z * 2 + other,
        )
        copy.start()
        core_copies[chunk] = copy
        sends.append(copy)

    def start_fib(chunk):
        core_copies[chunk].wait_recv()
        sum_core[chunk] = part[chunk, pl.ds(core * pieces, pieces)] + recv_core[chunk]
        fib_copies[chunk] = []
        for d in range(1, nfib):
            to = (fib + d) % nfib
            copy = remote(
                sum_core.at[chunk, pl.ds(to * nz, nz)], recv_fib.at[chunk, d - 1],
                fib_send.at[chunk, d], fib_recv.at[chunk, d], to, rest,
            )
            copy.start()
            fib_copies[chunk].append(copy)
            sends.append(copy)

    def start_z(chunk):
        total = sum_core[chunk, pl.ds(fib * nz, nz)]
        for d in range(1, nfib):
            fib_copies[chunk][d - 1].wait_recv()
            total = total + recv_fib[chunk, d - 1]
        sum_fib[chunk] = total
        z_copies[chunk] = []
        for d in range(1, nz):
            to = (z + d) % nz
            copy = remote(
                sum_fib.at[chunk, to], recv_z.at[chunk, d - 1],
                z_send.at[chunk, d], z_recv.at[chunk, d], fib, to * 2 + core,
            )
            copy.start()
            z_copies[chunk].append(copy)
            sends.append(copy)

    def finish(chunk):
        total = sum_fib[chunk, z]
        for d in range(1, nz):
            z_copies[chunk][d - 1].wait_recv()
            total = total + recv_z[chunk, d - 1]
        mine[chunk * piece : (chunk + 1) * piece, :] = total

    mine[...] = jnp.zeros_like(mine)
    fresh[...] = jnp.zeros_like(fresh)
    for chunk in range(chunks):
        multiply(chunk)
        start_core(chunk)
        if chunk >= 1:
            start_fib(chunk - 1)
        if chunk >= 2:
            start_z(chunk - 2)

    for copy in small:
        copy.wait_recv()
    if rows_two % 8 == 0:
        all_two = two_all[...].reshape(nfib * rows_two, rank)
    else:
        all_two = jnp.concatenate([two_all[f] for f in range(nfib)], axis=0)
    for q in range(nrest):
        three_cat[q * rows_three : (q + 1) * rows_three, :] = three_all[q]
    gram_v = gram_of(all_two) * gram_of(three_cat[...]) * gram_of(four)
    row_of = lax.broadcasted_iota(jnp.int32, (rank, rank), 0)
    col_of = lax.broadcasted_iota(jnp.int32, (rank, rank), 1)
    diag = jnp.sum(jnp.where(row_of == col_of, gram_v, 0.0), axis=1, keepdims=True)
    inverse = 1.0 / diag
    upper = jnp.where(col_of > row_of, gram_v, 0.0)
    scaled[...] = gram_v * inverse

    if chunks >= 2:
        start_z(chunks - 2)
    start_fib(chunks - 1)

    for i in range(rank):
        low_row = (i // BLOCK) * BLOCK
        spread[i, low_row:rank, :] = jnp.broadcast_to(scaled[low_row:rank, i : i + 1], (rank - low_row, LANES))

    xown_copy.wait()
    for chunk in range(chunks):
        fresh[chunk * piece : (chunk + 1) * piece, :] = xown[chunk]
    old_part = lax.dot_general(
        upper, fresh[...], (((1,), (1,)), ((), ())),
        precision=HIGHEST, preferred_element_type=jnp.float32,
    )

    start_z(chunks - 1)
    for chunk in range(chunks):
        finish(chunk)

    start = (mine[...].T - old_part) * inverse
    state = [start[b * BLOCK : (b + 1) * BLOCK] for b in range(nblocks)]
    for b in range(nblocks):
        rows = [state[b][k : k + 1] for k in range(BLOCK)]
        for k in range(BLOCK):
            i = b * BLOCK + k
            rows[k] = jnp.maximum(rows[k], 0.0)
            for later in range(k + 1, BLOCK):
                j = b * BLOCK + later
                rows[later] = rows[later] - spread[i, j : j + 1, :] * rows[k]
            fresh[i : i + 1, :] = rows[k]
            if b + 1 < nblocks:
                wide = jnp.broadcast_to(rows[k], (BLOCK, LANES))
                for later in range(b + 1, nblocks):
                    state[later] = state[later] - spread[i, later * BLOCK : (later + 1) * BLOCK, :] * wide
    own_rows = fresh[...].T
    for chunk in range(chunks):
        out[chunk, core, fib, z] = own_rows[chunk * piece : (chunk + 1) * piece]

    z_gather = []
    for d in range(1, nz):
        to = (z + d) % nz
        ref = out.at[:, core, fib, z]
        copy = remote(ref, ref, gz_send.at[d], gz_recv.at[d], fib, to * 2 + core)
        copy.start()
        z_gather.append(copy)
        sends.append(copy)
    fib_gather = []
    for dz in range(nz):
        if dz:
            z_gather[dz - 1].wait_recv()
        at = (z + nz - dz) % nz
        group = []
        for d in range(1, nfib):
            ref = out.at[:, core, fib, at]
            copy = remote(ref, ref, gf_send.at[dz, d], gf_recv.at[dz, d], (fib + d) % nfib, rest)
            copy.start()
            group.append(copy)
            sends.append(copy)
        fib_gather.append(group)
    core_gather = []
    for dz in range(nz):
        for copy in fib_gather[dz]:
            copy.wait_recv()
        at = (z + nz - dz) % nz
        ref = out.at[:, core, :, at]
        copy = remote(ref, ref, gc_send.at[dz], gc_recv.at[dz], fib, z * 2 + other)
        copy.start()
        core_gather.append(copy)
        sends.append(copy)

    def half(side):
        if piece % 8 == 0:
            return gram_of(out[:, side].reshape(chunks * pieces * piece, rank))
        for chunk in range(chunks):
            for f in range(nfib):
                for q in range(nz):
                    first = ((chunk * nfib + f) * nz + q) * piece
                    flat[first : first + piece, :] = out[chunk, side, f, q]
        return gram_of(flat[...])

    own_gram = half(core)
    for copy in core_gather:
        copy.wait_recv()
    gram_out[...] = own_gram + half(other)
    for copy in sends:
        copy.wait_send()


def per_device(tensor, factor_one, factor_two, factor_three, factor_four):
    nfib, nrest = lax.axis_size("fib"), lax.axis_size("rest")
    nz = nrest // 2
    mode_one, rank = factor_one.shape
    own = mode_one // (nfib * nrest)
    chunks = 4 if own % 32 == 0 else 1
    piece = own // chunks
    pieces = nfib * nz
    depth = tensor.shape[0] * tensor.shape[1] * tensor.shape[2]
    flat = tensor.reshape(depth, mode_one)
    ordered = (chunks, 2, nfib, nz, piece, rank)
    f32, bf16 = jnp.float32, jnp.bfloat16
    vmem = pl.BlockSpec(memory_space=pltpu.VMEM)
    anywhere = pl.BlockSpec(memory_space=pl.ANY)
    dma = pltpu.SemaphoreType.DMA
    out, gram = pl.pallas_call(
        functools.partial(kernel, (nfib, nrest, nz, chunks, piece)),
        out_shape=(
            jax.ShapeDtypeStruct(ordered, f32),
            jax.ShapeDtypeStruct((rank, rank), f32),
        ),
        in_specs=[anywhere, anywhere, vmem, vmem, vmem],
        out_specs=(vmem, vmem),
        scratch_shapes=[
            pltpu.VMEM((chunks, depth, mode_one // chunks), f32),
            pltpu.VMEM((chunks, piece, rank), f32),
            pltpu.VMEM((2 * rank, depth), bf16),
            pltpu.VMEM((nfib,) + factor_two.shape, f32),
            pltpu.VMEM((nrest,) + factor_three.shape, f32),
            pltpu.VMEM((nrest * factor_three.shape[0], rank), f32),
            pltpu.VMEM((chunks, 2 * pieces, piece, rank), f32),
            pltpu.VMEM((chunks, pieces, piece, rank), f32),
            pltpu.VMEM((chunks, pieces, piece, rank), f32),
            pltpu.VMEM((chunks, nfib - 1, nz, piece, rank), f32),
            pltpu.VMEM((chunks, nz, piece, rank), f32),
            pltpu.VMEM((chunks, nz - 1, piece, rank), f32),
            pltpu.VMEM((LANES, rank), f32),
            pltpu.VMEM((rank, rank), f32),
            pltpu.VMEM((rank, rank, LANES), f32),
            pltpu.VMEM((rank, LANES), f32),
            pltpu.VMEM((mode_one // 2, rank), f32),
            dma((chunks,)),
            dma,
            dma((nfib,)), dma((nfib,)),
            dma((nrest,)), dma((nrest,)),
            dma((chunks,)), dma((chunks,)),
            dma((chunks, nfib)), dma((chunks, nfib)),
            dma((chunks, nz)), dma((chunks, nz)),
            dma((nz,)), dma((nz,)),
            dma((nz, nfib)), dma((nz, nfib)),
            dma((nz,)), dma((nz,)),
        ],
        compiler_params=pltpu.CompilerParams(
            collective_id=0, has_side_effects=True, vmem_limit_bytes=56 * 1024 * 1024
        ),
    )(flat, factor_one.reshape(ordered), factor_two, factor_three, factor_four)
    return out.reshape(mode_one, rank), gram


def solution(mesh):
    return jax.shard_map(
        per_device,
        mesh=mesh,
        in_specs=(P("fib", "rest", None, None), P(), P("fib", None), P("rest", None), P()),
        out_specs=(P(), P()),
        check_vma=False,
    )
```

```python
import functools

import jax
import jax.numpy as jnp
from jax import lax
from jax.experimental import pallas as pl
from jax.experimental.pallas import tpu as pltpu
from jax.sharding import PartitionSpec as P

MESH = pl.DeviceIdType.MESH
HIGHEST = lax.Precision.HIGHEST
LANES = 128
BLOCK = 8


def split_bf16(value):
    high = value.astype(jnp.bfloat16)
    low = (value - high.astype(jnp.float32)).astype(jnp.bfloat16)
    return high, low


def gram_of(rows):
    return lax.dot_general(
        rows, rows, (((0,), (0,)), ((), ())),
        precision=HIGHEST, preferred_element_type=jnp.float32,
    )


def kernel(
    cfg, tensor, factor_one, factor_two, factor_three, factor_four, out,
    tbuf, xown, khatri_t, two_all, three_all, three_cat, part, recv_core, sum_core,
    recv_fib, sum_fib, recv_z, mine, scaled, spread, fresh,
    tensor_sem, xown_sem, two_send, two_recv, three_send, three_recv,
    core_send, core_recv, fib_send, fib_recv, z_send, z_recv,
    gz_send, gz_recv, gf_send, gf_recv, gc_send, gc_recv,
):
    nfib, nrest, nz, chunks, piece = cfg
    rank = factor_two.shape[1]
    fib = lax.axis_index("fib")
    rest = lax.axis_index("rest")
    core = rest % 2
    z = rest // 2
    other = 1 - core
    width = tensor.shape[1] // chunks
    pieces = nfib * nz
    nblocks = rank // BLOCK

    def remote(src, dst, send, recv, fib_to, rest_to):
        return pltpu.make_async_remote_copy(
            src_ref=src, dst_ref=dst, send_sem=send, recv_sem=recv,
            device_id=(fib_to, rest_to), device_id_type=MESH,
        )

    loads = []
    for chunk in range(chunks):
        copy = pltpu.make_async_copy(
            tensor.at[:, pl.ds(chunk * width, width)], tbuf.at[chunk], tensor_sem.at[chunk]
        )
        copy.start()
        loads.append(copy)
    xown_copy = pltpu.make_async_copy(factor_one.at[:, core, fib, z], xown, xown_sem)
    xown_copy.start()

    barrier = pltpu.get_barrier_semaphore()
    for d in range(1, nfib):
        pl.semaphore_signal(barrier, inc=1, device_id=((fib + d) % nfib, rest), device_id_type=MESH)
    for d in range(1, nrest):
        pl.semaphore_signal(barrier, inc=1, device_id=(fib, (rest + d) % nrest), device_id_type=MESH)

    two = factor_two[...]
    three = factor_three[...]
    four = factor_four[...]
    rows_two, rows_three, rows_four = two.shape[0], three.shape[0], four.shape[0]
    for i2 in range(rows_two):
        tile = jnp.concatenate(
            [(two[i2 : i2 + 1] * three[i3 : i3 + 1]) * four for i3 in range(rows_three)], axis=0
        )
        high, low = split_bf16(tile.T)
        span = rows_three * rows_four
        khatri_t[0:rank, i2 * span : (i2 + 1) * span] = high
        khatri_t[rank : 2 * rank, i2 * span : (i2 + 1) * span] = low

    two_all[fib] = two
    three_all[rest] = three
    small = []
    for d in range(1, nfib):
        small.append(remote(two_all.at[fib], two_all.at[fib], two_send.at[d], two_recv.at[d], (fib + d) % nfib, rest))
    for d in range(1, nrest):
        small.append(remote(three_all.at[rest], three_all.at[rest], three_send.at[d], three_recv.at[d], fib, (rest + d) % nrest))

    sends = list(small)

    def multiply(chunk):
        loads[chunk].wait()
        depth = tbuf.shape[1]
        step = min(depth, 512)
        total = None
        for k in range(0, depth, step):
            high, low = split_bf16(tbuf[chunk, k : k + step, :])
            weights = khatri_t[:, k : k + step]
            term = jnp.dot(weights, high, preferred_element_type=jnp.float32)
            term = term + jnp.dot(weights, low, preferred_element_type=jnp.float32)
            total = term if total is None else total + term
        value = (total[0:rank] + total[rank : 2 * rank]).T
        if piece % 8 == 0:
            part[chunk] = value.reshape(2 * pieces, piece, rank)
        else:
            for p in range(2 * pieces):
                part[chunk, p] = value[p * piece : (p + 1) * piece]

    core_copies, fib_copies, z_copies = {}, {}, {}

    def start_core(chunk):
        copy = remote(
            part.at[chunk, pl.ds(other * pieces, pieces)], recv_core.at[chunk],
            core_send.at[chunk], core_recv.at[chunk], fib, z * 2 + other,
        )
        copy.start()
        core_copies[chunk] = copy
        sends.append(copy)

    def start_fib(chunk):
        core_copies[chunk].wait_recv()
        sum_core[chunk] = part[chunk, pl.ds(core * pieces, pieces)] + recv_core[chunk]
        fib_copies[chunk] = []
        for d in range(1, nfib):
            to = (fib + d) % nfib
            copy = remote(
                sum_core.at[chunk, pl.ds(to * nz, nz)], recv_fib.at[chunk, d - 1],
                fib_send.at[chunk, d], fib_recv.at[chunk, d], to, rest,
            )
            copy.start()
            fib_copies[chunk].append(copy)
            sends.append(copy)

    def start_z(chunk):
        total = sum_core[chunk, pl.ds(fib * nz, nz)]
        for d in range(1, nfib):
            fib_copies[chunk][d - 1].wait_recv()
            total = total + recv_fib[chunk, d - 1]
        sum_fib[chunk] = total
        z_copies[chunk] = []
        for d in range(1, nz):
            to = (z + d) % nz
            copy = remote(
                sum_fib.at[chunk, to], recv_z.at[chunk, d - 1],
                z_send.at[chunk, d], z_recv.at[chunk, d], fib, to * 2 + core,
            )
            copy.start()
            z_copies[chunk].append(copy)
            sends.append(copy)

    def finish(chunk):
        total = sum_fib[chunk, z]
        for d in range(1, nz):
            z_copies[chunk][d - 1].wait_recv()
            total = total + recv_z[chunk, d - 1]
        mine[chunk * piece : (chunk + 1) * piece, :] = total

    mine[...] = jnp.zeros_like(mine)
    fresh[...] = jnp.zeros_like(fresh)
    for chunk in range(chunks):
        multiply(chunk)
        if chunk == 0:
            pl.semaphore_wait(barrier, nfib - 1 + nrest - 1)
        start_core(chunk)
        if chunk == 0:
            for copy in small:
                copy.start()
        if chunk >= 1:
            start_fib(chunk - 1)
        if chunk >= 2:
            start_z(chunk - 2)

    for copy in small:
        copy.wait_recv()
    if rows_two % 8 == 0:
        all_two = two_all[...].reshape(nfib * rows_two, rank)
    else:
        all_two = jnp.concatenate([two_all[f] for f in range(nfib)], axis=0)
    for q in range(nrest):
        three_cat[q * rows_three : (q + 1) * rows_three, :] = three_all[q]
    gram_v = gram_of(all_two) * gram_of(three_cat[...]) * gram_of(four)
    row_of = lax.broadcasted_iota(jnp.int32, (rank, rank), 0)
    col_of = lax.broadcasted_iota(jnp.int32, (rank, rank), 1)
    diag = jnp.sum(jnp.where(row_of == col_of, gram_v, 0.0), axis=1, keepdims=True)
    inverse = 1.0 / diag
    upper = jnp.where(col_of > row_of, gram_v, 0.0)
    scaled[...] = gram_v * inverse

    if chunks >= 2:
        start_z(chunks - 2)
    start_fib(chunks - 1)

    for i in range(rank):
        low_row = (i // BLOCK) * BLOCK
        spread[i, low_row:rank, :] = jnp.broadcast_to(scaled[low_row:rank, i : i + 1], (rank - low_row, LANES))

    start_z(chunks - 1)
    xown_copy.wait()
    for chunk in range(chunks):
        fresh[chunk * piece : (chunk + 1) * piece, :] = xown[chunk]
    old_part = lax.dot_general(
        upper, fresh[...], (((1,), (1,)), ((), ())),
        precision=HIGHEST, preferred_element_type=jnp.float32,
    )

    for chunk in range(chunks):
        finish(chunk)

    start = (mine[...].T - old_part) * inverse
    state = [start[b * BLOCK : (b + 1) * BLOCK] for b in range(nblocks)]
    for b in range(nblocks):
        rows = [jnp.broadcast_to(state[b][k : k + 1], (BLOCK, LANES)) for k in range(BLOCK)]
        for k in range(BLOCK):
            i = b * BLOCK + k
            rows[k] = jnp.maximum(rows[k], 0.0)
            for later in range(k + 1, BLOCK):
                j = b * BLOCK + later
                ratio = jnp.broadcast_to(spread[i, j : j + 1, :], (BLOCK, LANES))
                rows[later] = rows[later] - ratio * rows[k]
            fresh[i : i + 1, :] = rows[k][0:1]
            for later in range(b + 1, nblocks):
                state[later] = state[later] - spread[i, later * BLOCK : (later + 1) * BLOCK, :] * rows[k]
    own_rows = fresh[...].T
    for chunk in range(chunks):
        out[chunk, core, fib, z] = own_rows[chunk * piece : (chunk + 1) * piece]

    z_gather = []
    for d in range(1, nz):
        to = (z + d) % nz
        ref = out.at[:, core, fib, z]
        copy = remote(ref, ref, gz_send.at[d], gz_recv.at[d], fib, to * 2 + core)
        copy.start()
        z_gather.append(copy)
        sends.append(copy)
    fib_gather = []
    for dz in range(nz):
        if dz:
            z_gather[dz - 1].wait_recv()
        at = (z + nz - dz) % nz
        group = []
        for d in range(1, nfib):
            ref = out.at[:, core, fib, at]
            copy = remote(ref, ref, gf_send.at[dz, d], gf_recv.at[dz, d], (fib + d) % nfib, rest)
            copy.start()
            group.append(copy)
            sends.append(copy)
        fib_gather.append(group)
    core_gather = []
    for dz in range(nz):
        for copy in fib_gather[dz]:
            copy.wait_recv()
        at = (z + nz - dz) % nz
        ref = out.at[:, core, :, at]
        copy = remote(ref, ref, gc_send.at[dz], gc_recv.at[dz], fib, z * 2 + other)
        copy.start()
        core_gather.append(copy)
        sends.append(copy)

    for copy in core_gather:
        copy.wait_recv()
    for copy in sends:
        copy.wait_send()


def results(gathered, new_factor, gram, held, load_sem, store_sem):
    load = pltpu.make_async_copy(gathered, held, load_sem)
    load.start()
    load.wait()
    store = pltpu.make_async_copy(held, new_factor, store_sem)
    store.start()
    high, low = split_bf16(held[...])
    rank = held.shape[1]
    both = lax.dot_general(
        high, jnp.concatenate([high, low], axis=1), (((0,), (0,)), ((), ())),
        preferred_element_type=jnp.float32,
    )
    cross = both[:, rank:]
    gram[...] = both[:, :rank] + (cross + cross.T)
    store.wait()


def per_device(tensor, factor_one, factor_two, factor_three, factor_four):
    nfib, nrest = lax.axis_size("fib"), lax.axis_size("rest")
    nz = nrest // 2
    mode_one, rank = factor_one.shape
    own = mode_one // (nfib * nrest)
    chunks = 4 if own % 32 == 0 else 1
    piece = own // chunks
    pieces = nfib * nz
    depth = tensor.shape[0] * tensor.shape[1] * tensor.shape[2]
    flat = tensor.reshape(depth, mode_one)
    ordered = (chunks, 2, nfib, nz, piece, rank)
    f32, bf16 = jnp.float32, jnp.bfloat16
    vmem = pl.BlockSpec(memory_space=pltpu.VMEM)
    anywhere = pl.BlockSpec(memory_space=pl.ANY)
    dma = pltpu.SemaphoreType.DMA
    out = pl.pallas_call(
        functools.partial(kernel, (nfib, nrest, nz, chunks, piece)),
        out_shape=jax.ShapeDtypeStruct(ordered, f32),
        in_specs=[anywhere, anywhere, vmem, vmem, vmem],
        out_specs=vmem,
        scratch_shapes=[
            pltpu.VMEM((chunks, depth, mode_one // chunks), f32),
            pltpu.VMEM((chunks, piece, rank), f32),
            pltpu.VMEM((2 * rank, depth), bf16),
            pltpu.VMEM((nfib,) + factor_two.shape, f32),
            pltpu.VMEM((nrest,) + factor_three.shape, f32),
            pltpu.VMEM((nrest * factor_three.shape[0], rank), f32),
            pltpu.VMEM((chunks, 2 * pieces, piece, rank), f32),
            pltpu.VMEM((chunks, pieces, piece, rank), f32),
            pltpu.VMEM((chunks, pieces, piece, rank), f32),
            pltpu.VMEM((chunks, nfib - 1, nz, piece, rank), f32),
            pltpu.VMEM((chunks, nz, piece, rank), f32),
            pltpu.VMEM((chunks, nz - 1, piece, rank), f32),
            pltpu.VMEM((LANES, rank), f32),
            pltpu.VMEM((rank, rank), f32),
            pltpu.VMEM((rank, rank, LANES), f32),
            pltpu.VMEM((rank, LANES), f32),
            dma((chunks,)),
            dma,
            dma((nfib,)), dma((nfib,)),
            dma((nrest,)), dma((nrest,)),
            dma((chunks,)), dma((chunks,)),
            dma((chunks, nfib)), dma((chunks, nfib)),
            dma((chunks, nz)), dma((chunks, nz)),
            dma((nz,)), dma((nz,)),
            dma((nz, nfib)), dma((nz, nfib)),
            dma((nz,)), dma((nz,)),
        ],
        compiler_params=pltpu.CompilerParams(
            collective_id=0, has_side_effects=True, vmem_limit_bytes=56 * 1024 * 1024
        ),
    )(flat, factor_one.reshape(ordered), factor_two, factor_three, factor_four)
    return pl.pallas_call(
        results,
        out_shape=(
            jax.ShapeDtypeStruct((mode_one, rank), f32),
            jax.ShapeDtypeStruct((rank, rank), f32),
        ),
        in_specs=[anywhere],
        out_specs=(anywhere, vmem),
        scratch_shapes=[pltpu.VMEM((mode_one, rank), f32), dma, dma],
        compiler_params=pltpu.CompilerParams(vmem_limit_bytes=63 * 1024 * 1024),
    )(out.reshape(mode_one, rank))


def solution(mesh):
    return jax.shard_map(
        per_device,
        mesh=mesh,
        in_specs=(P("fib", "rest", None, None), P(), P("fib", None), P("rest", None), P()),
        out_specs=(P(), P()),
        check_vma=False,
    )
```

```python
import functools

import jax
import jax.numpy as jnp
from jax import lax
from jax.experimental import pallas as pl
from jax.experimental.pallas import tpu as pltpu
from jax.sharding import PartitionSpec as P

MESH = pl.DeviceIdType.MESH
HIGHEST = lax.Precision.HIGHEST
LANES = 128
BLOCK = 8


def split_bf16(value):
    high = value.astype(jnp.bfloat16)
    low = (value - high.astype(jnp.float32)).astype(jnp.bfloat16)
    return high, low


def gram_of(rows):
    return lax.dot_general(
        rows, rows, (((0,), (0,)), ((), ())),
        precision=HIGHEST, preferred_element_type=jnp.float32,
    )


def kernel(
    cfg, tensor, factor_one, factor_two, factor_three, factor_four, out,
    tbuf, xown, khatri_t, two_all, three_all, three_cat, part, recv_core, sum_core,
    recv_fib, sum_fib, recv_z, mine, scaled, spread, fresh, four_held, held,
    factor_sem, store_sem, tensor_sem, xown_sem, two_send, two_recv, three_send, three_recv,
    core_send, core_recv, fib_send, fib_recv, z_send, z_recv,
    gz_send, gz_recv, gf_send, gf_recv, gc_send, gc_recv,
):
    nfib, nrest, nz, chunks, piece = cfg
    rank = factor_two.shape[1]
    fib = lax.axis_index("fib")
    rest = lax.axis_index("rest")
    core = rest % 2
    z = rest // 2
    other = 1 - core
    width = tensor.shape[1] // chunks
    pieces = nfib * nz
    nblocks = rank // BLOCK

    def remote(src, dst, send, recv, fib_to, rest_to):
        return pltpu.make_async_remote_copy(
            src_ref=src, dst_ref=dst, send_sem=send, recv_sem=recv,
            device_id=(fib_to, rest_to), device_id_type=MESH,
        )

    factor_loads = [
        pltpu.make_async_copy(factor_two, two_all.at[fib], factor_sem.at[0]),
        pltpu.make_async_copy(factor_three, three_all.at[rest], factor_sem.at[1]),
        pltpu.make_async_copy(factor_four, four_held, factor_sem.at[2]),
    ]
    for copy in factor_loads:
        copy.start()
    loads = []
    for chunk in range(chunks):
        copy = pltpu.make_async_copy(
            tensor.at[:, pl.ds(chunk * width, width)], tbuf.at[chunk], tensor_sem.at[chunk]
        )
        loads.append(copy)
    for copy in loads[:2]:
        copy.start()
    barrier = pltpu.get_barrier_semaphore()
    for d in range(1, nfib):
        pl.semaphore_signal(barrier, inc=1, device_id=((fib + d) % nfib, rest), device_id_type=MESH)
    for d in range(1, nrest):
        pl.semaphore_signal(barrier, inc=1, device_id=(fib, (rest + d) % nrest), device_id_type=MESH)

    xown_copy = pltpu.make_async_copy(factor_one.at[:, core, fib, z], xown, xown_sem)
    xown_copy.start()

    for copy in factor_loads:
        copy.wait()

    two = two_all[fib]
    three = three_all[rest]
    four = four_held[...]
    rows_two, rows_three, rows_four = two.shape[0], three.shape[0], four.shape[0]
    for i2 in range(rows_two):
        tile = jnp.concatenate(
            [(two[i2 : i2 + 1] * three[i3 : i3 + 1]) * four for i3 in range(rows_three)], axis=0
        )
        high, low = split_bf16(tile.T)
        span = rows_three * rows_four
        khatri_t[0:rank, i2 * span : (i2 + 1) * span] = high
        khatri_t[rank : 2 * rank, i2 * span : (i2 + 1) * span] = low

    small = []
    for d in range(1, nfib):
        small.append(remote(two_all.at[fib], two_all.at[fib], two_send.at[d], two_recv.at[d], (fib + d) % nfib, rest))
    for d in range(1, nrest):
        small.append(remote(three_all.at[rest], three_all.at[rest], three_send.at[d], three_recv.at[d], fib, (rest + d) % nrest))

    sends = list(small)

    def multiply(chunk):
        loads[chunk].wait()
        if chunk + 2 < chunks:
            loads[chunk + 2].start()
        depth = tbuf.shape[1]
        step = min(depth, 512)
        total = None
        for k in range(0, depth, step):
            high, low = split_bf16(tbuf[chunk, k : k + step, :])
            weights = khatri_t[:, k : k + step]
            term = jnp.dot(weights, high, preferred_element_type=jnp.float32)
            term = term + jnp.dot(weights, low, preferred_element_type=jnp.float32)
            total = term if total is None else total + term
        value = (total[0:rank] + total[rank : 2 * rank]).T
        if piece % 8 == 0:
            part[chunk] = value.reshape(2 * pieces, piece, rank)
        else:
            for p in range(2 * pieces):
                part[chunk, p] = value[p * piece : (p + 1) * piece]

    core_copies, fib_copies, z_copies = {}, {}, {}

    def start_core(chunk):
        copy = remote(
            part.at[chunk, pl.ds(other * pieces, pieces)], recv_core.at[chunk],
            core_send.at[chunk], core_recv.at[chunk], fib, z * 2 + other,
        )
        copy.start()
        core_copies[chunk] = copy
        sends.append(copy)

    def start_fib(chunk):
        core_copies[chunk].wait_recv()
        sum_core[chunk] = part[chunk, pl.ds(core * pieces, pieces)] + recv_core[chunk]
        fib_copies[chunk] = []
        for d in range(1, nfib):
            to = (fib + d) % nfib
            copy = remote(
                sum_core.at[chunk, pl.ds(to * nz, nz)], recv_fib.at[chunk, d - 1],
                fib_send.at[chunk, d], fib_recv.at[chunk, d], to, rest,
            )
            copy.start()
            fib_copies[chunk].append(copy)
            sends.append(copy)

    def start_z(chunk):
        total = sum_core[chunk, pl.ds(fib * nz, nz)]
        for d in range(1, nfib):
            fib_copies[chunk][d - 1].wait_recv()
            total = total + recv_fib[chunk, d - 1]
        sum_fib[chunk] = total
        z_copies[chunk] = []
        for d in range(1, nz):
            to = (z + d) % nz
            copy = remote(
                sum_fib.at[chunk, to], recv_z.at[chunk, d - 1],
                z_send.at[chunk, d], z_recv.at[chunk, d], fib, to * 2 + core,
            )
            copy.start()
            z_copies[chunk].append(copy)
            sends.append(copy)

    def finish(chunk):
        total = sum_fib[chunk, z]
        for d in range(1, nz):
            z_copies[chunk][d - 1].wait_recv()
            total = total + recv_z[chunk, d - 1]
        mine[chunk * piece : (chunk + 1) * piece, :] = total

    mine[...] = jnp.zeros_like(mine)
    fresh[...] = jnp.zeros_like(fresh)
    for chunk in range(chunks):
        multiply(chunk)
        if chunk == 0:
            pl.semaphore_wait(barrier, nfib - 1 + nrest - 1)
        start_core(chunk)
        if chunk == 0:
            for copy in small:
                copy.start()
        if chunk >= 1:
            start_fib(chunk - 1)
        if chunk >= 2:
            start_z(chunk - 2)

    for copy in small:
        copy.wait_recv()
    if rows_two % 8 == 0:
        all_two = two_all[...].reshape(nfib * rows_two, rank)
    else:
        all_two = jnp.concatenate([two_all[f] for f in range(nfib)], axis=0)
    for q in range(nrest):
        three_cat[q * rows_three : (q + 1) * rows_three, :] = three_all[q]
    gram_v = gram_of(all_two) * gram_of(three_cat[...]) * gram_of(four)
    row_of = lax.broadcasted_iota(jnp.int32, (rank, rank), 0)
    col_of = lax.broadcasted_iota(jnp.int32, (rank, rank), 1)
    diag = jnp.sum(jnp.where(row_of == col_of, gram_v, 0.0), axis=1, keepdims=True)
    inverse = 1.0 / diag
    upper = jnp.where(col_of > row_of, gram_v, 0.0)
    scaled[...] = gram_v * inverse

    if chunks >= 2:
        start_z(chunks - 2)
    start_fib(chunks - 1)

    for i in range(rank):
        low_row = (i // BLOCK) * BLOCK
        spread[i, low_row:rank, :] = jnp.broadcast_to(scaled[low_row:rank, i : i + 1], (rank - low_row, LANES))

    start_z(chunks - 1)
    xown_copy.wait()
    for chunk in range(chunks):
        fresh[chunk * piece : (chunk + 1) * piece, :] = xown[chunk]
    old_part = lax.dot_general(
        upper, fresh[...], (((1,), (1,)), ((), ())),
        precision=HIGHEST, preferred_element_type=jnp.float32,
    )

    for chunk in range(chunks):
        finish(chunk)

    start = (mine[...].T - old_part) * inverse
    state = [start[b * BLOCK : (b + 1) * BLOCK] for b in range(nblocks)]
    for b in range(nblocks):
        rows = [jnp.broadcast_to(state[b][k : k + 1], (BLOCK, LANES)) for k in range(BLOCK)]
        for k in range(BLOCK):
            i = b * BLOCK + k
            rows[k] = jnp.maximum(rows[k], 0.0)
            for later in range(k + 1, BLOCK):
                j = b * BLOCK + later
                ratio = jnp.broadcast_to(spread[i, j : j + 1, :], (BLOCK, LANES))
                rows[later] = rows[later] - ratio * rows[k]
            fresh[i : i + 1, :] = rows[k][0:1]
            for later in range(b + 1, nblocks):
                state[later] = state[later] - spread[i, later * BLOCK : (later + 1) * BLOCK, :] * rows[k]
    own_rows = fresh[...].T
    for chunk in range(chunks):
        held[chunk, fib, z] = own_rows[chunk * piece : (chunk + 1) * piece]

    reduce_sends = list(sends)
    sends.clear()

    z_gather = []
    for d in range(1, nz):
        to = (z + d) % nz
        ref = held.at[:, fib, z]
        copy = remote(ref, ref, gz_send.at[d], gz_recv.at[d], fib, to * 2 + core)
        copy.start()
        z_gather.append(copy)
        sends.append(copy)
    fib_gather = []
    for dz in range(nz):
        if dz:
            z_gather[dz - 1].wait_recv()
        at = (z + nz - dz) % nz
        group = []
        for d in range(1, nfib):
            ref = held.at[:, fib, at]
            copy = remote(ref, ref, gf_send.at[dz, d], gf_recv.at[dz, d], (fib + d) % nfib, rest)
            copy.start()
            group.append(copy)
            sends.append(copy)
        fib_gather.append(group)
    core_gather, stores = [], []
    for dz in range(nz):
        for copy in fib_gather[dz]:
            copy.wait_recv()
        at = (z + nz - dz) % nz
        copy = remote(
            held.at[:, :, at], out.at[:, core, :, at], gc_send.at[dz], gc_recv.at[dz], fib, z * 2 + other
        )
        copy.start()
        core_gather.append(copy)
        sends.append(copy)
        store = pltpu.make_async_copy(held.at[:, :, at], out.at[:, core, :, at], store_sem.at[dz])
        store.start()
        stores.append(store)
        if dz == 0:
            for copy in reduce_sends:
                copy.wait_send()

    for copy in stores:
        copy.wait()
    for copy in sends:
        copy.wait_send()
    for copy in core_gather:
        copy.wait_recv()


def results(gathered, new_factor, gram, held, load_sem, store_sem):
    parts = load_sem.shape[0]
    rows, rank = held.shape
    step = rows // parts
    loads, stores = [], []
    for k in range(parts):
        span = pl.ds(k * step, step)
        loads.append(pltpu.make_async_copy(gathered.at[span], held.at[span], load_sem.at[k]))
        stores.append(pltpu.make_async_copy(held.at[span], new_factor.at[span], store_sem.at[k]))
        loads[k].start()
    both = None
    for k in range(parts):
        loads[k].wait()
        stores[k].start()
        high, low = split_bf16(held[k * step : (k + 1) * step])
        term = lax.dot_general(
            high, jnp.concatenate([high, low], axis=1), (((0,), (0,)), ((), ())),
            preferred_element_type=jnp.float32,
        )
        both = term if both is None else both + term
    cross = both[:, rank:]
    gram[...] = both[:, :rank] + (cross + cross.T)
    for copy in stores:
        copy.wait()


def per_device(tensor, factor_one, factor_two, factor_three, factor_four):
    nfib, nrest = lax.axis_size("fib"), lax.axis_size("rest")
    nz = nrest // 2
    mode_one, rank = factor_one.shape
    own = mode_one // (nfib * nrest)
    chunks = 4 if own % 32 == 0 else 1
    piece = own // chunks
    pieces = nfib * nz
    depth = tensor.shape[0] * tensor.shape[1] * tensor.shape[2]
    flat = tensor.reshape(depth, mode_one)
    ordered = (chunks, 2, nfib, nz, piece, rank)
    f32, bf16 = jnp.float32, jnp.bfloat16
    vmem = pl.BlockSpec(memory_space=pltpu.VMEM)
    anywhere = pl.BlockSpec(memory_space=pl.ANY)
    dma = pltpu.SemaphoreType.DMA
    out = pl.pallas_call(
        functools.partial(kernel, (nfib, nrest, nz, chunks, piece)),
        out_shape=jax.ShapeDtypeStruct(ordered, f32),
        in_specs=[anywhere] * 5,
        out_specs=anywhere,
        scratch_shapes=[
            pltpu.VMEM((chunks, depth, mode_one // chunks), f32),
            pltpu.VMEM((chunks, piece, rank), f32),
            pltpu.VMEM((2 * rank, depth), bf16),
            pltpu.VMEM((nfib,) + factor_two.shape, f32),
            pltpu.VMEM((nrest,) + factor_three.shape, f32),
            pltpu.VMEM((nrest * factor_three.shape[0], rank), f32),
            pltpu.VMEM((chunks, 2 * pieces, piece, rank), f32),
            pltpu.VMEM((chunks, pieces, piece, rank), f32),
            pltpu.VMEM((chunks, pieces, piece, rank), f32),
            pltpu.VMEM((chunks, nfib - 1, nz, piece, rank), f32),
            pltpu.VMEM((chunks, nz, piece, rank), f32),
            pltpu.VMEM((chunks, nz - 1, piece, rank), f32),
            pltpu.VMEM((LANES, rank), f32),
            pltpu.VMEM((rank, rank), f32),
            pltpu.VMEM((rank, rank, LANES), f32),
            pltpu.VMEM((rank, LANES), f32),
            pltpu.VMEM(factor_four.shape, f32),
            pltpu.VMEM((chunks, nfib, nz, piece, rank), f32),
            dma((3,)), dma((nz,)),
            dma((chunks,)),
            dma,
            dma((nfib,)), dma((nfib,)),
            dma((nrest,)), dma((nrest,)),
            dma((chunks,)), dma((chunks,)),
            dma((chunks, nfib)), dma((chunks, nfib)),
            dma((chunks, nz)), dma((chunks, nz)),
            dma((nz,)), dma((nz,)),
            dma((nz, nfib)), dma((nz, nfib)),
            dma((nz,)), dma((nz,)),
        ],
        compiler_params=pltpu.CompilerParams(
            collective_id=0, has_side_effects=True, vmem_limit_bytes=56 * 1024 * 1024
        ),
    )(flat, factor_one.reshape(ordered), factor_two, factor_three, factor_four)
    return pl.pallas_call(
        results,
        out_shape=(
            jax.ShapeDtypeStruct((mode_one, rank), f32),
            jax.ShapeDtypeStruct((rank, rank), f32),
        ),
        in_specs=[anywhere],
        out_specs=(anywhere, vmem),
        scratch_shapes=[pltpu.VMEM((mode_one, rank), f32), dma((4,)), dma((4,))],
        compiler_params=pltpu.CompilerParams(vmem_limit_bytes=63 * 1024 * 1024),
    )(out.reshape(mode_one, rank))


def solution(mesh):
    return jax.shard_map(
        per_device,
        mesh=mesh,
        in_specs=(P("fib", "rest", None, None), P(), P("fib", None), P("rest", None), P()),
        out_specs=(P(), P()),
        check_vma=False,
    )
```

```python
import functools

import jax
import jax.numpy as jnp
from jax import lax
from jax.experimental import pallas as pl
from jax.experimental.pallas import tpu as pltpu
from jax.sharding import PartitionSpec as P

MESH = pl.DeviceIdType.MESH
HIGHEST = lax.Precision.HIGHEST
LANES = 128
BLOCK = 8


def split_bf16(value):
    high = value.astype(jnp.bfloat16)
    low = (value - high.astype(jnp.float32)).astype(jnp.bfloat16)
    return high, low


def gram_of(rows):
    return lax.dot_general(
        rows, rows, (((0,), (0,)), ((), ())),
        precision=HIGHEST, preferred_element_type=jnp.float32,
    )


def kernel(
    cfg, tensor, factor_one, factor_two, factor_three, factor_four, out,
    tbuf, xown, khatri_t, two_all, three_all, three_cat, part, recv_core, sum_core,
    recv_fib, sum_fib, recv_z, mine, scaled, spread, fresh, four_held, held, acc,
    factor_sem, store_sem, tensor_sem, xown_sem, two_send, two_recv, three_send, three_recv,
    core_send, core_recv, fib_send, fib_recv, z_send, z_recv,
    gz_send, gz_recv, gf_send, gf_recv, gc_send, gc_recv,
):
    nfib, nrest, nz, chunks, piece = cfg
    rank = factor_two.shape[1]
    fib = lax.axis_index("fib")
    rest = lax.axis_index("rest")
    core = rest % 2
    z = rest // 2
    other = 1 - core
    width = tensor.shape[1] // chunks
    pieces = nfib * nz
    nblocks = rank // BLOCK

    def remote(src, dst, send, recv, fib_to, rest_to):
        return pltpu.make_async_remote_copy(
            src_ref=src, dst_ref=dst, send_sem=send, recv_sem=recv,
            device_id=(fib_to, rest_to), device_id_type=MESH,
        )

    factor_loads = [
        pltpu.make_async_copy(factor_two, two_all.at[fib], factor_sem.at[0]),
        pltpu.make_async_copy(factor_three, three_all.at[rest], factor_sem.at[1]),
        pltpu.make_async_copy(factor_four, four_held, factor_sem.at[2]),
    ]
    for copy in factor_loads:
        copy.start()
    loads = []
    for chunk in range(chunks):
        copy = pltpu.make_async_copy(
            tensor.at[:, pl.ds(chunk * width, width)], tbuf.at[chunk], tensor_sem.at[chunk]
        )
        loads.append(copy)
    for copy in loads[:2]:
        copy.start()
    barrier = pltpu.get_barrier_semaphore()
    for d in range(1, nfib):
        pl.semaphore_signal(barrier, inc=1, device_id=((fib + d) % nfib, rest), device_id_type=MESH)
    for d in range(1, nrest):
        pl.semaphore_signal(barrier, inc=1, device_id=(fib, (rest + d) % nrest), device_id_type=MESH)

    xown_copy = pltpu.make_async_copy(factor_one.at[:, core, fib, z], xown, xown_sem)
    xown_copy.start()

    for copy in factor_loads:
        copy.wait()

    three = three_all[rest]
    four = four_held[...]
    rows_two, rows_three, rows_four = factor_two.shape[0], three.shape[0], four.shape[0]
    span = rows_three * rows_four

    def fill(i2, carry):
        row = two_all[fib, pl.ds(i2, 1), :]
        tile = jnp.concatenate(
            [(row * three[i3 : i3 + 1]) * four for i3 in range(rows_three)], axis=0
        )
        high, low = split_bf16(tile.T)
        at = pl.ds(pl.multiple_of(i2 * span, span), span)
        khatri_t[0:rank, at] = high
        khatri_t[rank : 2 * rank, at] = low
        return carry

    lax.fori_loop(0, rows_two, fill, 0)

    small = []
    for d in range(1, nfib):
        small.append(remote(two_all.at[fib], two_all.at[fib], two_send.at[d], two_recv.at[d], (fib + d) % nfib, rest))
    for d in range(1, nrest):
        small.append(remote(three_all.at[rest], three_all.at[rest], three_send.at[d], three_recv.at[d], fib, (rest + d) % nrest))

    sends = list(small)

    def multiply(chunk):
        loads[chunk].wait()
        if chunk + 2 < chunks:
            loads[chunk + 2].start()
        depth = tbuf.shape[1]
        step = min(depth, 512)
        acc[...] = jnp.zeros_like(acc)

        def accumulate(k, carry):
            at = pl.ds(pl.multiple_of(k * step, step), step)
            high, low = split_bf16(tbuf[chunk, at, :])
            weights = khatri_t[:, at]
            term = jnp.dot(weights, high, preferred_element_type=jnp.float32)
            term = term + jnp.dot(weights, low, preferred_element_type=jnp.float32)
            acc[...] += term
            return carry

        lax.fori_loop(0, depth // step, accumulate, 0)
        total = acc[...]
        value = (total[0:rank] + total[rank : 2 * rank]).T
        if piece % 8 == 0:
            part[chunk] = value.reshape(2 * pieces, piece, rank)
        else:
            for p in range(2 * pieces):
                part[chunk, p] = value[p * piece : (p + 1) * piece]

    core_copies, fib_copies, z_copies = {}, {}, {}

    def start_core(chunk):
        copy = remote(
            part.at[chunk, pl.ds(other * pieces, pieces)], recv_core.at[chunk],
            core_send.at[chunk], core_recv.at[chunk], fib, z * 2 + other,
        )
        copy.start()
        core_copies[chunk] = copy
        sends.append(copy)

    def start_fib(chunk):
        core_copies[chunk].wait_recv()
        sum_core[chunk] = part[chunk, pl.ds(core * pieces, pieces)] + recv_core[chunk]
        fib_copies[chunk] = []
        for d in range(1, nfib):
            to = (fib + d) % nfib
            copy = remote(
                sum_core.at[chunk, pl.ds(to * nz, nz)], recv_fib.at[chunk, d - 1],
                fib_send.at[chunk, d], fib_recv.at[chunk, d], to, rest,
            )
            copy.start()
            fib_copies[chunk].append(copy)
            sends.append(copy)

    def start_z(chunk):
        total = sum_core[chunk, pl.ds(fib * nz, nz)]
        for d in range(1, nfib):
            fib_copies[chunk][d - 1].wait_recv()
            total = total + recv_fib[chunk, d - 1]
        sum_fib[chunk] = total
        z_copies[chunk] = []
        for d in range(1, nz):
            to = (z + d) % nz
            copy = remote(
                sum_fib.at[chunk, to], recv_z.at[chunk, d - 1],
                z_send.at[chunk, d], z_recv.at[chunk, d], fib, to * 2 + core,
            )
            copy.start()
            z_copies[chunk].append(copy)
            sends.append(copy)

    def finish(chunk):
        total = sum_fib[chunk, z]
        for d in range(1, nz):
            z_copies[chunk][d - 1].wait_recv()
            total = total + recv_z[chunk, d - 1]
        mine[chunk * piece : (chunk + 1) * piece, :] = total

    mine[...] = jnp.zeros_like(mine)
    fresh[...] = jnp.zeros_like(fresh)
    for chunk in range(chunks):
        multiply(chunk)
        if chunk == 0:
            pl.semaphore_wait(barrier, nfib - 1 + nrest - 1)
        start_core(chunk)
        if chunk == 0:
            for copy in small:
                copy.start()
        if chunk >= 1:
            start_fib(chunk - 1)
        if chunk >= 2:
            start_z(chunk - 2)

    for copy in small:
        copy.wait_recv()
    if rows_two % 8 == 0:
        all_two = two_all[...].reshape(nfib * rows_two, rank)
    else:
        all_two = jnp.concatenate([two_all[f] for f in range(nfib)], axis=0)
    for q in range(nrest):
        three_cat[q * rows_three : (q + 1) * rows_three, :] = three_all[q]
    gram_v = gram_of(all_two) * gram_of(three_cat[...]) * gram_of(four)
    row_of = lax.broadcasted_iota(jnp.int32, (rank, rank), 0)
    col_of = lax.broadcasted_iota(jnp.int32, (rank, rank), 1)
    diag = jnp.sum(jnp.where(row_of == col_of, gram_v, 0.0), axis=1, keepdims=True)
    inverse = 1.0 / diag
    upper = jnp.where(col_of > row_of, gram_v, 0.0)
    scaled[...] = gram_v * inverse

    if chunks >= 2:
        start_z(chunks - 2)
    start_fib(chunks - 1)

    for i in range(rank):
        low_row = (i // BLOCK) * BLOCK
        spread[i, low_row:rank, :] = jnp.broadcast_to(scaled[low_row:rank, i : i + 1], (rank - low_row, LANES))

    start_z(chunks - 1)
    xown_copy.wait()
    for chunk in range(chunks):
        fresh[chunk * piece : (chunk + 1) * piece, :] = xown[chunk]
    old_part = lax.dot_general(
        upper, fresh[...], (((1,), (1,)), ((), ())),
        precision=HIGHEST, preferred_element_type=jnp.float32,
    )

    for chunk in range(chunks):
        finish(chunk)

    start = (mine[...].T - old_part) * inverse
    state = [start[b * BLOCK : (b + 1) * BLOCK] for b in range(nblocks)]
    for b in range(nblocks):
        rows = [jnp.broadcast_to(state[b][k : k + 1], (BLOCK, LANES)) for k in range(BLOCK)]
        for k in range(BLOCK):
            i = b * BLOCK + k
            rows[k] = jnp.maximum(rows[k], 0.0)
            for later in range(k + 1, BLOCK):
                j = b * BLOCK + later
                ratio = jnp.broadcast_to(spread[i, j : j + 1, :], (BLOCK, LANES))
                rows[later] = rows[later] - ratio * rows[k]
            fresh[i : i + 1, :] = rows[k][0:1]
            for later in range(b + 1, nblocks):
                state[later] = state[later] - spread[i, later * BLOCK : (later + 1) * BLOCK, :] * rows[k]
    own_rows = fresh[...].T
    for chunk in range(chunks):
        held[chunk, fib, z] = own_rows[chunk * piece : (chunk + 1) * piece]

    reduce_sends = list(sends)
    sends.clear()

    z_gather = []
    for d in range(1, nz):
        to = (z + d) % nz
        ref = held.at[:, fib, z]
        copy = remote(ref, ref, gz_send.at[d], gz_recv.at[d], fib, to * 2 + core)
        copy.start()
        z_gather.append(copy)
        sends.append(copy)
    fib_gather = []
    for dz in range(nz):
        if dz:
            z_gather[dz - 1].wait_recv()
        at = (z + nz - dz) % nz
        group = []
        for d in range(1, nfib):
            ref = held.at[:, fib, at]
            copy = remote(ref, ref, gf_send.at[dz, d], gf_recv.at[dz, d], (fib + d) % nfib, rest)
            copy.start()
            group.append(copy)
            sends.append(copy)
        fib_gather.append(group)
    core_gather, stores = [], []
    for dz in range(nz):
        for copy in fib_gather[dz]:
            copy.wait_recv()
        at = (z + nz - dz) % nz
        copy = remote(
            held.at[:, :, at], out.at[:, core, :, at], gc_send.at[dz], gc_recv.at[dz], fib, z * 2 + other
        )
        copy.start()
        core_gather.append(copy)
        sends.append(copy)
        store = pltpu.make_async_copy(held.at[:, :, at], out.at[:, core, :, at], store_sem.at[dz])
        store.start()
        stores.append(store)
        if dz == 0:
            for copy in reduce_sends:
                copy.wait_send()

    for copy in stores:
        copy.wait()
    for copy in sends:
        copy.wait_send()
    for copy in core_gather:
        copy.wait_recv()


def results(gathered, new_factor, gram, held, load_sem, store_sem):
    parts = load_sem.shape[0]
    rows, rank = held.shape
    step = rows // parts
    loads, stores = [], []
    for k in range(parts):
        span = pl.ds(k * step, step)
        loads.append(pltpu.make_async_copy(gathered.at[span], held.at[span], load_sem.at[k]))
        stores.append(pltpu.make_async_copy(held.at[span], new_factor.at[span], store_sem.at[k]))
        loads[k].start()
    both = None
    for k in range(parts):
        loads[k].wait()
        stores[k].start()
        high, low = split_bf16(held[k * step : (k + 1) * step])
        term = lax.dot_general(
            high, jnp.concatenate([high, low], axis=1), (((0,), (0,)), ((), ())),
            preferred_element_type=jnp.float32,
        )
        both = term if both is None else both + term
    cross = both[:, rank:]
    gram[...] = both[:, :rank] + (cross + cross.T)
    for copy in stores:
        copy.wait()


def per_device(tensor, factor_one, factor_two, factor_three, factor_four):
    nfib, nrest = lax.axis_size("fib"), lax.axis_size("rest")
    nz = nrest // 2
    mode_one, rank = factor_one.shape
    own = mode_one // (nfib * nrest)
    chunks = 4 if own % 32 == 0 else 1
    piece = own // chunks
    pieces = nfib * nz
    depth = tensor.shape[0] * tensor.shape[1] * tensor.shape[2]
    flat = tensor.reshape(depth, mode_one)
    ordered = (chunks, 2, nfib, nz, piece, rank)
    f32, bf16 = jnp.float32, jnp.bfloat16
    vmem = pl.BlockSpec(memory_space=pltpu.VMEM)
    anywhere = pl.BlockSpec(memory_space=pl.ANY)
    dma = pltpu.SemaphoreType.DMA
    out = pl.pallas_call(
        functools.partial(kernel, (nfib, nrest, nz, chunks, piece)),
        out_shape=jax.ShapeDtypeStruct(ordered, f32),
        in_specs=[anywhere] * 5,
        out_specs=anywhere,
        scratch_shapes=[
            pltpu.VMEM((chunks, depth, mode_one // chunks), f32),
            pltpu.VMEM((chunks, piece, rank), f32),
            pltpu.VMEM((2 * rank, depth), bf16),
            pltpu.VMEM((nfib,) + factor_two.shape, f32),
            pltpu.VMEM((nrest,) + factor_three.shape, f32),
            pltpu.VMEM((nrest * factor_three.shape[0], rank), f32),
            pltpu.VMEM((chunks, 2 * pieces, piece, rank), f32),
            pltpu.VMEM((chunks, pieces, piece, rank), f32),
            pltpu.VMEM((chunks, pieces, piece, rank), f32),
            pltpu.VMEM((chunks, nfib - 1, nz, piece, rank), f32),
            pltpu.VMEM((chunks, nz, piece, rank), f32),
            pltpu.VMEM((chunks, nz - 1, piece, rank), f32),
            pltpu.VMEM((LANES, rank), f32),
            pltpu.VMEM((rank, rank), f32),
            pltpu.VMEM((rank, rank, LANES), f32),
            pltpu.VMEM((rank, LANES), f32),
            pltpu.VMEM(factor_four.shape, f32),
            pltpu.VMEM((chunks, nfib, nz, piece, rank), f32),
            pltpu.VMEM((2 * rank, mode_one // chunks), f32),
            dma((3,)), dma((nz,)),
            dma((chunks,)),
            dma,
            dma((nfib,)), dma((nfib,)),
            dma((nrest,)), dma((nrest,)),
            dma((chunks,)), dma((chunks,)),
            dma((chunks, nfib)), dma((chunks, nfib)),
            dma((chunks, nz)), dma((chunks, nz)),
            dma((nz,)), dma((nz,)),
            dma((nz, nfib)), dma((nz, nfib)),
            dma((nz,)), dma((nz,)),
        ],
        compiler_params=pltpu.CompilerParams(
            collective_id=0, has_side_effects=True, vmem_limit_bytes=56 * 1024 * 1024
        ),
    )(flat, factor_one.reshape(ordered), factor_two, factor_three, factor_four)
    return pl.pallas_call(
        results,
        out_shape=(
            jax.ShapeDtypeStruct((mode_one, rank), f32),
            jax.ShapeDtypeStruct((rank, rank), f32),
        ),
        in_specs=[anywhere],
        out_specs=(anywhere, vmem),
        scratch_shapes=[pltpu.VMEM((mode_one, rank), f32), dma((1,)), dma((1,))],
        compiler_params=pltpu.CompilerParams(vmem_limit_bytes=63 * 1024 * 1024),
    )(out.reshape(mode_one, rank))


def solution(mesh):
    return jax.shard_map(
        per_device,
        mesh=mesh,
        in_specs=(P("fib", "rest", None, None), P(), P("fib", None), P("rest", None), P()),
        out_specs=(P(), P()),
        check_vma=False,
    )
```

```python
import functools

import jax
import jax.numpy as jnp
from jax import lax
from jax.experimental import pallas as pl
from jax.experimental.pallas import tpu as pltpu
from jax.sharding import PartitionSpec as P

MESH = pl.DeviceIdType.MESH
HIGHEST = lax.Precision.HIGHEST
LANES = 128
BLOCK = 8


def split_bf16(value):
    high = value.astype(jnp.bfloat16)
    low = (value - high.astype(jnp.float32)).astype(jnp.bfloat16)
    return high, low


def gram_of(rows):
    return lax.dot_general(
        rows, rows, (((0,), (0,)), ((), ())),
        precision=HIGHEST, preferred_element_type=jnp.float32,
    )


def kernel(
    cfg, tensor, factor_one, factor_two, factor_three, factor_four, out,
    tbuf, xown, khatri_t, two_all, three_all, three_cat, part, recv_core, sum_core,
    recv_fib, sum_fib, recv_z, mine, scaled, spread, fresh, four_held, held, acc, recv_direct,
    direct_send, direct_recv, factor_sem, store_sem, tensor_sem, xown_sem, two_send, two_recv, three_send, three_recv,
    core_send, core_recv, fib_send, fib_recv, z_send, z_recv,
    gz_send, gz_recv, gf_send, gf_recv, gc_send, gc_recv,
):
    nfib, nrest, nz, chunks, piece = cfg
    rank = factor_two.shape[1]
    fib = lax.axis_index("fib")
    rest = lax.axis_index("rest")
    core = rest % 2
    z = rest // 2
    other = 1 - core
    width = tensor.shape[1] // chunks
    pieces = nfib * nz
    nblocks = rank // BLOCK

    def remote(src, dst, send, recv, fib_to, rest_to):
        return pltpu.make_async_remote_copy(
            src_ref=src, dst_ref=dst, send_sem=send, recv_sem=recv,
            device_id=(fib_to, rest_to), device_id_type=MESH,
        )

    factor_loads = [
        pltpu.make_async_copy(factor_two, two_all.at[fib], factor_sem.at[0]),
        pltpu.make_async_copy(factor_three, three_all.at[rest], factor_sem.at[1]),
        pltpu.make_async_copy(factor_four, four_held, factor_sem.at[2]),
    ]
    for copy in factor_loads:
        copy.start()
    loads = []
    for chunk in range(chunks):
        copy = pltpu.make_async_copy(
            tensor.at[:, pl.ds(chunk * width, width)], tbuf.at[chunk], tensor_sem.at[chunk]
        )
        loads.append(copy)
    for copy in loads[:2]:
        copy.start()
    barrier = pltpu.get_barrier_semaphore()
    for df in range(nfib):
        for dz in range(nz):
            to = ((z + dz) % nz) * 2
            if df or dz:
                pl.semaphore_signal(
                    barrier, inc=1, device_id=((fib + df) % nfib, to + core), device_id_type=MESH
                )
            if df == 0:
                pl.semaphore_signal(barrier, inc=1, device_id=(fib, to + other), device_id_type=MESH)

    xown_copy = pltpu.make_async_copy(factor_one.at[:, core, fib, z], xown, xown_sem)
    xown_copy.start()

    for copy in factor_loads:
        copy.wait()

    three = three_all[rest]
    four = four_held[...]
    rows_two, rows_three, rows_four = factor_two.shape[0], three.shape[0], four.shape[0]
    span = rows_three * rows_four

    def fill(i2, carry):
        row = two_all[fib, pl.ds(i2, 1), :]
        tile = jnp.concatenate(
            [(row * three[i3 : i3 + 1]) * four for i3 in range(rows_three)], axis=0
        )
        high, low = split_bf16(tile.T)
        at = pl.ds(pl.multiple_of(i2 * span, span), span)
        khatri_t[0:rank, at] = high
        khatri_t[rank : 2 * rank, at] = low
        return carry

    lax.fori_loop(0, rows_two, fill, 0)

    small = []
    for d in range(1, nfib):
        small.append(remote(two_all.at[fib], two_all.at[fib], two_send.at[d], two_recv.at[d], (fib + d) % nfib, rest))
    for d in range(1, nrest):
        small.append(remote(three_all.at[rest], three_all.at[rest], three_send.at[d], three_recv.at[d], fib, (rest + d) % nrest))

    sends = list(small)

    def multiply(chunk):
        loads[chunk].wait()
        if chunk + 2 < chunks:
            loads[chunk + 2].start()
        depth = tbuf.shape[1]
        step = min(depth, 512)
        acc[...] = jnp.zeros_like(acc)

        def accumulate(k, carry):
            at = pl.ds(pl.multiple_of(k * step, step), step)
            high, low = split_bf16(tbuf[chunk, at, :])
            weights = khatri_t[:, at]
            term = jnp.dot(weights, high, preferred_element_type=jnp.float32)
            term = term + jnp.dot(weights, low, preferred_element_type=jnp.float32)
            acc[...] += term
            return carry

        lax.fori_loop(0, depth // step, accumulate, 0)
        total = acc[...]
        value = (total[0:rank] + total[rank : 2 * rank]).T
        if piece % 8 == 0:
            part[chunk] = value.reshape(2 * pieces, piece, rank)
        else:
            for p in range(2 * pieces):
                part[chunk, p] = value[p * piece : (p + 1) * piece]

    core_copies, fib_copies, z_copies = {}, {}, {}

    def start_core(chunk):
        copy = remote(
            part.at[chunk, pl.ds(other * pieces, pieces)], recv_core.at[chunk],
            core_send.at[chunk], core_recv.at[chunk], fib, z * 2 + other,
        )
        copy.start()
        core_copies[chunk] = copy
        sends.append(copy)

    def start_fib(chunk):
        core_copies[chunk].wait_recv()
        sum_core[chunk] = part[chunk, pl.ds(core * pieces, pieces)] + recv_core[chunk]
        fib_copies[chunk] = []
        for d in range(1, nfib):
            to = (fib + d) % nfib
            copy = remote(
                sum_core.at[chunk, pl.ds(to * nz, nz)], recv_fib.at[chunk, d - 1],
                fib_send.at[chunk, d], fib_recv.at[chunk, d], to, rest,
            )
            copy.start()
            fib_copies[chunk].append(copy)
            sends.append(copy)

    def start_z(chunk):
        total = sum_core[chunk, pl.ds(fib * nz, nz)]
        for d in range(1, nfib):
            fib_copies[chunk][d - 1].wait_recv()
            total = total + recv_fib[chunk, d - 1]
        sum_fib[chunk] = total
        z_copies[chunk] = []
        for d in range(1, nz):
            to = (z + d) % nz
            copy = remote(
                sum_fib.at[chunk, to], recv_z.at[chunk, d - 1],
                z_send.at[chunk, d], z_recv.at[chunk, d], fib, to * 2 + core,
            )
            copy.start()
            z_copies[chunk].append(copy)
            sends.append(copy)

    def finish(chunk):
        total = sum_fib[chunk, z]
        for d in range(1, nz):
            z_copies[chunk][d - 1].wait_recv()
            total = total + recv_z[chunk, d - 1]
        mine[chunk * piece : (chunk + 1) * piece, :] = total

    direct = []

    def start_direct(chunk):
        core_copies[chunk].wait_recv()
        sum_core[chunk] = part[chunk, pl.ds(core * pieces, pieces)] + recv_core[chunk]
        for df in range(nfib):
            for dz in range(nz):
                if df == 0 and dz == 0:
                    continue
                fib_to, z_to, slot = (fib + df) % nfib, (z + dz) % nz, df * nz + dz
                copy = remote(
                    sum_core.at[chunk, fib_to * nz + z_to], recv_direct.at[slot],
                    direct_send.at[slot], direct_recv.at[slot], fib_to, z_to * 2 + core,
                )
                copy.start()
                direct.append(copy)
                sends.append(copy)

    def finish_direct(chunk):
        total = sum_core[chunk, fib * nz + z]
        for slot in range(1, pieces):
            direct[slot - 1].wait_recv()
            total = total + recv_direct[slot]
        mine[chunk * piece : (chunk + 1) * piece, :] = total

    mine[...] = jnp.zeros_like(mine)
    fresh[...] = jnp.zeros_like(fresh)
    for chunk in range(chunks):
        multiply(chunk)
        if chunk == 0:
            pl.semaphore_wait(barrier, pieces - 1 + nz)
        start_core(chunk)
        if chunk == 0:
            for copy in small:
                copy.start()
        if chunk >= 1:
            start_fib(chunk - 1)
        if chunk >= 2:
            start_z(chunk - 2)

    for copy in small:
        copy.wait_recv()
    if rows_two % 8 == 0:
        all_two = two_all[...].reshape(nfib * rows_two, rank)
    else:
        all_two = jnp.concatenate([two_all[f] for f in range(nfib)], axis=0)
    for q in range(nrest):
        three_cat[q * rows_three : (q + 1) * rows_three, :] = three_all[q]
    gram_v = gram_of(all_two) * gram_of(three_cat[...]) * gram_of(four)
    row_of = lax.broadcasted_iota(jnp.int32, (rank, rank), 0)
    col_of = lax.broadcasted_iota(jnp.int32, (rank, rank), 1)
    diag = jnp.sum(jnp.where(row_of == col_of, gram_v, 0.0), axis=1, keepdims=True)
    inverse = 1.0 / diag
    upper = jnp.where(col_of > row_of, gram_v, 0.0)
    scaled[...] = gram_v * inverse

    if chunks >= 2:
        start_z(chunks - 2)
    start_direct(chunks - 1)

    for i in range(rank):
        low_row = (i // BLOCK) * BLOCK
        spread[i, low_row:rank, :] = jnp.broadcast_to(scaled[low_row:rank, i : i + 1], (rank - low_row, LANES))

    xown_copy.wait()
    for chunk in range(chunks):
        fresh[chunk * piece : (chunk + 1) * piece, :] = xown[chunk]
    old_part = lax.dot_general(
        upper, fresh[...], (((1,), (1,)), ((), ())),
        precision=HIGHEST, preferred_element_type=jnp.float32,
    )

    for chunk in range(chunks - 1):
        finish(chunk)
    finish_direct(chunks - 1)

    start = (mine[...].T - old_part) * inverse
    state = [start[b * BLOCK : (b + 1) * BLOCK] for b in range(nblocks)]
    for b in range(nblocks):
        rows = [jnp.broadcast_to(state[b][k : k + 1], (BLOCK, LANES)) for k in range(BLOCK)]
        for k in range(BLOCK):
            i = b * BLOCK + k
            rows[k] = jnp.maximum(rows[k], 0.0)
            for later in range(k + 1, BLOCK):
                j = b * BLOCK + later
                ratio = jnp.broadcast_to(spread[i, j : j + 1, :], (BLOCK, LANES))
                rows[later] = rows[later] - ratio * rows[k]
            fresh[i : i + 1, :] = rows[k][0:1]
            for later in range(b + 1, nblocks):
                state[later] = state[later] - spread[i, later * BLOCK : (later + 1) * BLOCK, :] * rows[k]
    own_rows = fresh[...].T
    for chunk in range(chunks):
        held[chunk, fib, z] = own_rows[chunk * piece : (chunk + 1) * piece]

    reduce_sends = list(sends)
    sends.clear()

    z_gather = []
    for d in range(1, nz):
        to = (z + d) % nz
        ref = held.at[:, fib, z]
        copy = remote(ref, ref, gz_send.at[d], gz_recv.at[d], fib, to * 2 + core)
        copy.start()
        z_gather.append(copy)
        sends.append(copy)
    fib_gather = []
    for dz in range(nz):
        if dz:
            z_gather[dz - 1].wait_recv()
        at = (z + nz - dz) % nz
        group = []
        for d in range(1, nfib):
            ref = held.at[:, fib, at]
            copy = remote(ref, ref, gf_send.at[dz, d], gf_recv.at[dz, d], (fib + d) % nfib, rest)
            copy.start()
            group.append(copy)
            sends.append(copy)
        fib_gather.append(group)
    core_gather, stores = [], []
    for dz in range(nz):
        for copy in fib_gather[dz]:
            copy.wait_recv()
        at = (z + nz - dz) % nz
        copy = remote(
            held.at[:, :, at], out.at[:, core, :, at], gc_send.at[dz], gc_recv.at[dz], fib, z * 2 + other
        )
        copy.start()
        core_gather.append(copy)
        sends.append(copy)
        store = pltpu.make_async_copy(held.at[:, :, at], out.at[:, core, :, at], store_sem.at[dz])
        store.start()
        stores.append(store)
        if dz == 0:
            for copy in reduce_sends:
                copy.wait_send()

    for copy in stores:
        copy.wait()
    for copy in sends:
        copy.wait_send()
    for copy in core_gather:
        copy.wait_recv()


def results(gathered, new_factor, gram, held, load_sem, store_sem):
    parts = load_sem.shape[0]
    rows, rank = held.shape
    step = rows // parts
    loads, stores = [], []
    for k in range(parts):
        span = pl.ds(k * step, step)
        loads.append(pltpu.make_async_copy(gathered.at[span], held.at[span], load_sem.at[k]))
        stores.append(pltpu.make_async_copy(held.at[span], new_factor.at[span], store_sem.at[k]))
        loads[k].start()
    both = None
    for k in range(parts):
        loads[k].wait()
        stores[k].start()
        high, low = split_bf16(held[k * step : (k + 1) * step])
        term = lax.dot_general(
            high, jnp.concatenate([high, low], axis=1), (((0,), (0,)), ((), ())),
            preferred_element_type=jnp.float32,
        )
        both = term if both is None else both + term
    cross = both[:, rank:]
    gram[...] = both[:, :rank] + (cross + cross.T)
    for copy in stores:
        copy.wait()


def per_device(tensor, factor_one, factor_two, factor_three, factor_four):
    nfib, nrest = lax.axis_size("fib"), lax.axis_size("rest")
    nz = nrest // 2
    mode_one, rank = factor_one.shape
    own = mode_one // (nfib * nrest)
    chunks = 4 if own % 32 == 0 else 1
    piece = own // chunks
    pieces = nfib * nz
    depth = tensor.shape[0] * tensor.shape[1] * tensor.shape[2]
    flat = tensor.reshape(depth, mode_one)
    ordered = (chunks, 2, nfib, nz, piece, rank)
    f32, bf16 = jnp.float32, jnp.bfloat16
    vmem = pl.BlockSpec(memory_space=pltpu.VMEM)
    anywhere = pl.BlockSpec(memory_space=pl.ANY)
    dma = pltpu.SemaphoreType.DMA
    out = pl.pallas_call(
        functools.partial(kernel, (nfib, nrest, nz, chunks, piece)),
        out_shape=jax.ShapeDtypeStruct(ordered, f32),
        in_specs=[anywhere] * 5,
        out_specs=anywhere,
        scratch_shapes=[
            pltpu.VMEM((chunks, depth, mode_one // chunks), f32),
            pltpu.VMEM((chunks, piece, rank), f32),
            pltpu.VMEM((2 * rank, depth), bf16),
            pltpu.VMEM((nfib,) + factor_two.shape, f32),
            pltpu.VMEM((nrest,) + factor_three.shape, f32),
            pltpu.VMEM((nrest * factor_three.shape[0], rank), f32),
            pltpu.VMEM((chunks, 2 * pieces, piece, rank), f32),
            pltpu.VMEM((chunks, pieces, piece, rank), f32),
            pltpu.VMEM((chunks, pieces, piece, rank), f32),
            pltpu.VMEM((chunks, nfib - 1, nz, piece, rank), f32),
            pltpu.VMEM((chunks, nz, piece, rank), f32),
            pltpu.VMEM((chunks, nz - 1, piece, rank), f32),
            pltpu.VMEM((LANES, rank), f32),
            pltpu.VMEM((rank, rank), f32),
            pltpu.VMEM((rank, rank, LANES), f32),
            pltpu.VMEM((rank, LANES), f32),
            pltpu.VMEM(factor_four.shape, f32),
            pltpu.VMEM((chunks, nfib, nz, piece, rank), f32),
            pltpu.VMEM((2 * rank, mode_one // chunks), f32),
            pltpu.VMEM((pieces, piece, rank), f32),
            dma((pieces,)), dma((pieces,)),
            dma((3,)), dma((nz,)),
            dma((chunks,)),
            dma,
            dma((nfib,)), dma((nfib,)),
            dma((nrest,)), dma((nrest,)),
            dma((chunks,)), dma((chunks,)),
            dma((chunks, nfib)), dma((chunks, nfib)),
            dma((chunks, nz)), dma((chunks, nz)),
            dma((nz,)), dma((nz,)),
            dma((nz, nfib)), dma((nz, nfib)),
            dma((nz,)), dma((nz,)),
        ],
        compiler_params=pltpu.CompilerParams(
            collective_id=0, has_side_effects=True, vmem_limit_bytes=56 * 1024 * 1024
        ),
    )(flat, factor_one.reshape(ordered), factor_two, factor_three, factor_four)
    return pl.pallas_call(
        results,
        out_shape=(
            jax.ShapeDtypeStruct((mode_one, rank), f32),
            jax.ShapeDtypeStruct((rank, rank), f32),
        ),
        in_specs=[anywhere],
        out_specs=(anywhere, vmem),
        scratch_shapes=[pltpu.VMEM((mode_one, rank), f32), dma((1,)), dma((1,))],
        compiler_params=pltpu.CompilerParams(vmem_limit_bytes=63 * 1024 * 1024),
    )(out.reshape(mode_one, rank))


def solution(mesh):
    return jax.shard_map(
        per_device,
        mesh=mesh,
        in_specs=(P("fib", "rest", None, None), P(), P("fib", None), P("rest", None), P()),
        out_specs=(P(), P()),
        check_vma=False,
    )
```
